32 devices in a mesh: dp: 4 (over x, core), vocab: 8 (over z, y).
Axes of the slice: x: 2, y: 2, z: 4, core: 2. Of those that a mesh axis runs over, the one named last changes fastest.
Arguments:
- head_input: bfloat16 [512, 8192], P(('dp', 'vocab')), may hold values from -250 to 250
- body_input: bfloat16 [512, 8192], P(('dp', 'vocab')), may hold values from -6 to 6
- head_weight: bfloat16 [16384, 8192], P('vocab'), may hold values from -0.0625 to 0.0625
- gate_weight: bfloat16 [8192, 14336], P('dp', 'vocab'), may hold values from -0.0625 to 0.0625
- up_weight: bfloat16 [8192, 14336], P('dp', 'vocab'), may hold values from -0.0625 to 0.0625
- down_weight: bfloat16 [8192, 14336], P('dp', 'vocab'), may hold values from -0.046875 to 0.046875
- tile_ids: int32 [1024, 128], P(('dp', 'vocab')), may hold values from 0 to 16383, as said below
- tile_probs: bfloat16 [1024, 128], P(('dp', 'vocab')), may hold values from 0 to 1, as said below
- tile_slot: int32 [512], P('dp'), may hold values from 0 to 255, as said below
Outputs:
- input_grad: bfloat16 [512, 8192], P('dp', 'vocab')
The draws below stay inside these ranges and needn't reach their ends.
Inputs may be any that keep to these rules, and one draw needn't show every extreme that they name: `tile_ids`: each stored slot lists 128 distinct token ids. `tile_probs`: in every slot the probabilities are positive and sum to at most 0.95. `tile_slot`: A group's store of 256 slots lies on the devices of one index of dp in order of vocab, 32 slots a device; rows of a group use distinct slots, so half of the slots hold no row's tile and are never read; in every group all 32 slots of some device are used, and which device varies.
All inputs are finite; a program needn't handle non-finite values.
Results may differ from the reference program's by a relative error of at most 0.02.
Values may be sent and summed in bfloat16 or wider, within the bound.
A program may use at most 128 MiB of HBM per device.

```python
import jax
import jax.numpy as jnp
from jax import lax

D = 8192
FF = 14336
VOCAB = 16384
K = 128
MICRO = 2
MB_ROWS = 64
LOSS_SCALE = 1024
ROWS = 512
STORE = 256
SLOTS = 32
VOCAB_DEV = 2048
FF_DEV = 1792
N_VOCAB = 8


def draw_head_input(key, part):
    first = jax.random.fold_in(key, 0)
    values = jnp.clip(jax.random.normal(first, (ROWS, D), jnp.float32), -6.0, 6.0)
    values = values * 3.0
    return values.astype(jnp.bfloat16)


def draw_tile_ids(key, part):
    count = 2 * ROWS
    first, second = jax.random.split(key)
    popular = jax.random.randint(first, (VOCAB,), 0, 4) * 4096
    noise = jax.random.randint(second, (count, VOCAB), 0, 4096)
    scores = (noise + popular[None, :]) * VOCAB + jnp.arange(VOCAB, dtype=jnp.int32)[None, :]
    return lax.top_k(scores, K)[1].astype(jnp.int32)


def draw_tile_probs(key, part):
    count = 2 * ROWS
    first, second = jax.random.split(key)
    levels = jax.random.uniform(first, (count, K), jnp.float32, 0.1, 1.0)
    factor = jax.random.uniform(second, (count, 1), jnp.float32, 0.2, 1.0)
    return (0.95 / K * levels * factor).astype(jnp.bfloat16)


def draw_tile_slot(key, part):
    group_rows = MICRO * MB_ROWS
    groups = ROWS // group_rows

    def one_group(index):
        group_key = jax.random.fold_in(key, index)
        busy_key, score_key, perm_key = jax.random.split(group_key, 3)
        busy = jax.random.randint(busy_key, (), 0, STORE // SLOTS)
        places = jnp.arange(STORE, dtype=jnp.int32)
        forced = (places // SLOTS == busy) | (places == 0) | (places == STORE - 1)
        scores = jax.random.randint(score_key, (STORE,), 0, 1 << 20) + jnp.where(forced, 0, 1 << 20)
        order = jnp.argsort(scores * STORE + places, stable=True).astype(jnp.int32)
        shuffle = jax.random.permutation(perm_key, group_rows)
        return jnp.zeros((group_rows,), jnp.int32).at[shuffle].set(order[:group_rows])
    return jax.vmap(one_group)(jnp.arange(groups, dtype=jnp.int32)).reshape(ROWS)


def steps_of(rng, extent, cuts, least, high):
    def one(dim, shards_of):
        steps = jax.random.uniform(jax.random.fold_in(jax.random.fold_in(rng, 6), dim), (shards_of,), jnp.float32, least / len(cuts), high / len(cuts))
        return jnp.repeat(jnp.exp(steps), extent[dim] // shards_of).reshape((-1,) + (1,) * (len(extent) - dim - 1))

    loudness = one(*cuts[0])
    for cut in cuts[1:]:
        loudness = loudness * one(*cut)
    return loudness


def bell_draw(rng, extent, width, most, pieces=(), kind=jnp.bfloat16):
    values = width * jax.random.normal(rng, extent, jnp.float32)
    if pieces:
        values = values * steps_of(rng, extent, pieces, -0.22, 0.18)
    return jnp.clip(values, -most, most).astype(kind)


def setup_inputs(seed: int = 0) -> dict:
    splits = jax.random.split(jax.random.key(seed), 10)
    return {
        "head_input": draw_head_input(jax.random.fold_in(splits[9], 71), 0),
        "body_input": bell_draw(splits[1], (ROWS, D), 1.0, 6.0, ((0, 32),)),
        "head_weight": bell_draw(splits[2], (VOCAB, D), D ** -0.5, 0.0625, ((0, 8),)),
        "gate_weight": bell_draw(splits[3], (D, FF), D ** -0.5, 0.0625, ((0, 4), (1, 8))),
        "up_weight": bell_draw(splits[4], (D, FF), D ** -0.5, 0.0625, ((0, 4), (1, 8))),
        "down_weight": bell_draw(splits[5], (D, FF), FF ** -0.5, 0.046875, ((0, 4), (1, 8))),
        "tile_ids": draw_tile_ids(jax.random.fold_in(splits[9], 71), 0),
        "tile_probs": draw_tile_probs(jax.random.fold_in(splits[9], 71), 0),
        "tile_slot": draw_tile_slot(jax.random.fold_in(splits[9], 71), 0),
    }


def group_grad(head_rows, body_rows, slots, store_ids, store_probs, head_weight, gate_weight, up_weight, down_weight):
    count = head_rows.shape[0]
    row_ids = store_ids[slots]
    row_probs = store_probs[slots].astype(jnp.float32)
    lines = jnp.broadcast_to(jnp.arange(count, dtype=jnp.int32)[:, None], row_ids.shape)
    teacher = jnp.zeros((count, VOCAB), jnp.float32).at[lines, row_ids].add(row_probs)
    picked = jnp.zeros((count, VOCAB), jnp.bool_).at[lines, row_ids].set(True)
    tail_mass = 1.0 - lax.optimization_barrier(jnp.sum(row_probs, axis=1, keepdims=True))
    logits = jnp.dot(head_rows, head_weight.T, preferred_element_type=jnp.float32)
    row_max = lax.optimization_barrier(jnp.max(logits, axis=1, keepdims=True))
    rest = jnp.where(picked, -1e+30, logits)
    rest_max = lax.optimization_barrier(jnp.max(rest, axis=1, keepdims=True))
    top_sum = lax.optimization_barrier(jnp.sum(jnp.where(picked, jnp.exp(logits - row_max), 0.0), axis=1, keepdims=True))
    rest_exp = jnp.where(picked, 0.0, jnp.exp(rest - rest_max))
    rest_sum = lax.optimization_barrier(jnp.sum(rest_exp, axis=1, keepdims=True))
    total = top_sum + rest_sum * jnp.exp(rest_max - row_max)
    student = jnp.exp(logits - row_max) / total
    spread = rest_exp / rest_sum
    top_share = top_sum / total
    logit_grad = (LOSS_SCALE * (student * (1.0 - tail_mass) + jnp.where(picked, tail_mass * student - teacher, -tail_mass * top_share * spread))).astype(jnp.bfloat16)

    def head_block(carry, index):
        grad_block = lax.dynamic_slice_in_dim(logit_grad, index * VOCAB_DEV, VOCAB_DEV, 1)
        weight_block = lax.dynamic_slice_in_dim(head_weight, index * VOCAB_DEV, VOCAB_DEV, 0)
        part = jnp.dot(grad_block, weight_block, preferred_element_type=jnp.float32).astype(jnp.bfloat16)
        part = lax.optimization_barrier(part)
        return (carry + part.astype(jnp.float32), None)
    head_sum, _ = lax.scan(head_block, jnp.zeros((count, D), jnp.float32), jnp.arange(N_VOCAB, dtype=jnp.int32))
    head_grad = head_sum.astype(jnp.bfloat16)
    gate_act = jnp.dot(body_rows, gate_weight, preferred_element_type=jnp.float32)
    up_act = jnp.dot(body_rows, up_weight, preferred_element_type=jnp.float32)
    down_grad = jnp.dot(head_grad, down_weight, preferred_element_type=jnp.float32)
    sigma = jax.nn.sigmoid(gate_act)
    gate_grad = (down_grad * up_act * sigma * (1.0 + gate_act * (1.0 - sigma))).astype(jnp.bfloat16)
    up_grad = (down_grad * gate_act * sigma).astype(jnp.bfloat16)

    def body_block(carry, index):
        gate_part = lax.dynamic_slice_in_dim(gate_grad, index * FF_DEV, FF_DEV, 1)
        up_part = lax.dynamic_slice_in_dim(up_grad, index * FF_DEV, FF_DEV, 1)
        gate_cols = lax.dynamic_slice_in_dim(gate_weight, index * FF_DEV, FF_DEV, 1)
        up_cols = lax.dynamic_slice_in_dim(up_weight, index * FF_DEV, FF_DEV, 1)
        part = jnp.dot(gate_part, gate_cols.T, preferred_element_type=jnp.float32) + jnp.dot(up_part, up_cols.T, preferred_element_type=jnp.float32)
        part = lax.optimization_barrier(part.astype(jnp.bfloat16))
        return (carry + part.astype(jnp.float32), None)
    branch, _ = lax.scan(body_block, jnp.zeros((count, D), jnp.float32), jnp.arange(N_VOCAB, dtype=jnp.int32))
    return (head_grad.astype(jnp.float32) + branch).astype(jnp.bfloat16)

def reference(head_input, body_input, head_weight, gate_weight, up_weight, down_weight, tile_ids, tile_probs, tile_slot):
    group_rows = MICRO * MB_ROWS
    groups = head_input.shape[0] // group_rows

    def one_group(index):
        head_rows = lax.dynamic_slice_in_dim(head_input, index * group_rows, group_rows, 0)
        body_rows = lax.dynamic_slice_in_dim(body_input, index * group_rows, group_rows, 0)
        slots = lax.dynamic_slice_in_dim(tile_slot, index * group_rows, group_rows, 0)
        store_ids = lax.dynamic_slice_in_dim(tile_ids, index * STORE, STORE, 0)
        store_probs = lax.dynamic_slice_in_dim(tile_probs, index * STORE, STORE, 0)
        return group_grad(head_rows, body_rows, slots, store_ids, store_probs, head_weight, gate_weight, up_weight, down_weight)
    result = lax.map(one_group, jnp.arange(groups, dtype=jnp.int32))
    return result.reshape(head_input.shape[0], D)
```

```python
import functools

import jax
import jax.numpy as jnp
from jax import lax
from jax.experimental import pallas as pl
from jax.experimental.pallas import tpu as pltpu
from jax.sharding import PartitionSpec as P

LOSS_SCALE = 1024
LANES = 128
MESH = pl.DeviceIdType.MESH
VMEM = pltpu.VMEM
F32 = jnp.float32
BF16 = jnp.bfloat16
DMA = pltpu.SemaphoreType.DMA


def params(ident, mib=48):
    return pltpu.CompilerParams(
        collective_id=ident, has_side_effects=True, vmem_limit_bytes=mib * 1024 * 1024
    )


def remote(src, dst, send, recv, where):
    return pltpu.make_async_remote_copy(
        src_ref=src,
        dst_ref=dst,
        send_sem=send,
        recv_sem=recv,
        device_id=where,
        device_id_type=MESH,
    )


def greet(peers):
    barrier = pltpu.get_barrier_semaphore()
    for peer in peers:
        pl.semaphore_signal(barrier, inc=1, device_id=peer, device_id_type=MESH)
    pl.semaphore_wait(barrier, len(peers))


def grid_peers(nv):
    v = lax.axis_index("vocab")
    nz = nv // 2
    z, y = v // 2, lax.rem(v, 2)
    along = [{"vocab": lax.rem(z + s, nz) * 2 + y} for s in range(1, nz)]
    return z, y, along, {"vocab": z * 2 + 1 - y}


def spread_start(nv, source, slot, zs, zr, ys, yr):
    z, y, along, partner = grid_peers(nv)
    mine = z * 2 + y
    copies = []
    for s in range(1, nv // 2):
        copies.append(
            remote(source, slot(mine), zs.at[s - 1], zr.at[s - 1], along[s - 1])
        )
    copies.append(remote(source, slot(mine), ys.at[0], yr.at[0], partner))
    for copy in copies:
        copy.start()
    return copies


def spread_forward(nv, s, slot, zs, zr, ys, yr):
    z, y, along, partner = grid_peers(nv)
    nz = nv // 2
    came = lax.rem(z - s + nz, nz) * 2 + y
    remote(slot(came), slot(came), zs.at[s - 1], zr.at[s - 1], along[s - 1]).wait_recv()
    copy = remote(slot(came), slot(came), ys.at[s], yr.at[s], partner)
    copy.start()
    return copy


def spread_finish(nv, copies, slot, ys, yr):
    z, y, _, partner = grid_peers(nv)
    nz = nv // 2
    for s in range(nz):
        theirs = lax.rem(z - s + nz, nz) * 2 + 1 - y
        remote(slot(theirs), slot(theirs), ys.at[s], yr.at[s], partner).wait_recv()
    for copy in copies:
        copy.wait_send()


def intake_kernel(
    nd, nv, vocab_rows,
    head_ref, body_ref, ids_ref, probs_ref, slot_ref,
    rows_ref, cols_ref, enc_ref, tail_ref,
    ids_all, probs_all, hi_s, lo_s, p_s,
    hzs, hzr, hys, hyr, ts, tr, us, ur, bs, br,
):
    d = lax.axis_index("dp")
    v = lax.axis_index("vocab")
    nz = nv // 2
    z, y, along, partner = grid_peers(nv)
    width = body_ref.shape[1] // nd
    everyone = [{"vocab": lax.rem(v + s, nv)} for s in range(1, nv)]
    others = [{"dp": lax.rem(d + s, nd)} for s in range(1, nd)]
    greet(everyone + others)
    small = []
    for s in range(1, nv):
        small.append(remote(ids_ref, ids_all.at[v], ts.at[s - 1], tr.at[s - 1], everyone[s - 1]))
        small.append(
            remote(probs_ref, probs_all.at[v], us.at[s - 1], ur.at[s - 1], everyone[s - 1])
        )
    for copy in small:
        copy.start()
    heads = spread_start(nv, head_ref, lambda k: rows_ref.at[k], hzs, hzr, hys, hyr)
    crossing = []
    for s in range(1, nd):
        to = lax.rem(d + s, nd)
        part = body_ref.at[:, pl.ds(pl.multiple_of(to * width, width), width)]
        crossing.append(remote(part, cols_ref.at[d], bs.at[s - 1], br.at[s - 1], others[s - 1]))
    for copy in crossing:
        copy.start()
    rows_ref[v] = head_ref[...]
    cols_ref[d] = body_ref[:, pl.ds(pl.multiple_of(d * width, width), width)]
    ids_all[v] = ids_ref[...]
    probs_all[v] = probs_ref[...]
    for s in range(1, nv):
        came = lax.rem(v - s + nv, nv)
        remote(ids_ref, ids_all.at[came], ts.at[s - 1], tr.at[s - 1], everyone[0]).wait_recv()
        remote(probs_ref, probs_all.at[came], us.at[s - 1], ur.at[s - 1], everyone[0]).wait_recv()

    count = slot_ref.shape[0]
    slots = ids_ref.shape[0]
    hi = jnp.zeros((count, LANES), F32)
    lo = jnp.zeros((count, LANES), F32)
    pr = jnp.zeros((count, LANES), F32)
    wanted = slot_ref[...]
    place = lax.broadcasted_iota(jnp.int32, (count, slots), 1)
    for k in range(nv):
        pick = jnp.where(place + k * slots == wanted, 1.0, 0.0).astype(BF16)
        ids = ids_all[k]
        top = lax.shift_right_logical(ids, 7).astype(F32).astype(BF16)
        low = lax.bitwise_and(ids, 127).astype(F32).astype(BF16)
        hi = hi + jnp.dot(pick, top, preferred_element_type=F32)
        lo = lo + jnp.dot(pick, low, preferred_element_type=F32)
        pr = pr + jnp.dot(pick, probs_all[k], preferred_element_type=F32)
    tail_ref[...] = 1.0 - jnp.sum(pr, axis=1, keepdims=True)
    nh = vocab_rows // LANES
    hi_s[...] = hi - (v * nh).astype(F32)
    lo_s[...] = lo
    p_s[...] = pr
    up_high = lax.broadcasted_iota(jnp.int32, (nh, LANES), 0).astype(F32)
    up_low = lax.broadcasted_iota(jnp.int32, (LANES, LANES), 0).astype(F32)

    def eight(step, carry):
        at = pl.multiple_of(step * 8, 8)
        hi8 = hi_s[pl.ds(at, 8), :]
        lo8 = lo_s[pl.ds(at, 8), :]
        p8 = p_s[pl.ds(at, 8), :]
        for j in range(8):
            hot = up_high == hi8[j : j + 1]
            low = jnp.where(up_low == lo8[j : j + 1], 1.0, 0.0).astype(BF16)
            both = jnp.concatenate(
                [jnp.where(hot, p8[j : j + 1], 0.0), jnp.where(hot, 1.0, 0.0)], axis=0
            ).astype(BF16)
            found = lax.dot_general(
                both, low, (((1,), (1,)), ((), ())), preferred_element_type=F32
            )
            enc_ref[at + j] = jnp.where(found[nh:] > 0.5, found[:nh], -1.0)
        return carry

    steps = count // 8
    bounds = [steps * s // nz for s in range(nz + 1)]
    for s in range(nz):
        lax.fori_loop(bounds[s], bounds[s + 1], eight, 0)
        if s + 1 < nz:
            heads.append(
                spread_forward(nv, s + 1, lambda k: rows_ref.at[k], hzs, hzr, hys, hyr)
            )
    spread_finish(nv, heads, lambda k: rows_ref.at[k], hys, hyr)
    for s in range(1, nd):
        came = lax.rem(d - s + nd, nd)
        remote(
            cols_ref.at[came], cols_ref.at[came], bs.at[s - 1], br.at[s - 1], others[0]
        ).wait_recv()
    for copy in crossing + small:
        copy.wait_send()


def intake(nd, nv, vocab_rows, head_input, body_input, ids, probs, slot):
    m, width = head_input.shape
    slots, k = ids.shape
    count = slot.shape[0]
    nz = nv // 2
    return pl.pallas_call(
        functools.partial(intake_kernel, nd, nv, vocab_rows),
        out_shape=(
            jax.ShapeDtypeStruct((nv, m, width), BF16),
            jax.ShapeDtypeStruct((nd, m, width // nd), BF16),
            jax.ShapeDtypeStruct((count, vocab_rows // LANES, LANES), F32),
            jax.ShapeDtypeStruct((count, 1), F32),
        ),
        in_specs=[pl.BlockSpec(memory_space=VMEM)] * 5,
        out_specs=(pl.BlockSpec(memory_space=VMEM),) * 4,
        scratch_shapes=[
            VMEM((nv, slots, k), jnp.int32),
            VMEM((nv, slots, k), BF16),
            VMEM((count, k), F32),
            VMEM((count, k), F32),
            VMEM((count, k), F32),
            DMA((nz,)), DMA((nz,)), DMA((nz,)), DMA((nz,)),
            DMA((nv,)), DMA((nv,)), DMA((nv,)), DMA((nv,)),
            DMA((nd,)), DMA((nd,)),
        ],
        compiler_params=params(0),
    )(head_input, body_input, ids, probs, slot[:, None])


def stats_kernel(nv, logits_ref, enc_ref, tail_ref, grad_ref, mine, got, ss, sr):
    v = lax.axis_index("vocab")
    everyone = [{"vocab": lax.rem(v + s, nv)} for s in range(1, nv)]
    greet(everyone)
    count = logits_ref.shape[0]
    logits = logits_ref[...]
    picked = enc_ref[...] >= 0.0
    top_max = jnp.max(logits, axis=1, keepdims=True)
    rest = jnp.where(picked, -1e30, logits)
    low_max = jnp.max(rest, axis=1, keepdims=True)
    top = jnp.sum(jnp.where(picked, jnp.exp(logits - top_max), 0.0), axis=1, keepdims=True)
    low = jnp.sum(jnp.where(picked, 0.0, jnp.exp(rest - low_max)), axis=1, keepdims=True)
    lane = lax.broadcasted_iota(jnp.int32, (count, LANES), 1)
    packed = jnp.where(
        lane == 0, top_max, jnp.where(lane == 1, top, jnp.where(lane == 2, low_max, low))
    )
    mine[...] = packed.T[0:8]
    got[v] = mine[...]
    copies = [
        remote(mine, got.at[v], ss.at[s - 1], sr.at[s - 1], everyone[s - 1])
        for s in range(1, nv)
    ]
    for copy in copies:
        copy.start()
    for s in range(1, nv):
        came = lax.rem(v - s + nv, nv)
        remote(mine, got.at[came], ss.at[s - 1], sr.at[s - 1], everyone[0]).wait_recv()
    every = [got[k] for k in range(nv)]
    row_max = functools.reduce(jnp.maximum, [e[0:1] for e in every])
    rest_max = functools.reduce(jnp.maximum, [e[2:3] for e in every])
    top_sum = sum(e[1:2] * jnp.exp(e[0:1] - row_max) for e in every)
    rest_sum = sum(e[3:4] * jnp.exp(e[2:3] - rest_max) for e in every)
    total = top_sum + rest_sum * jnp.exp(rest_max - row_max)
    line = lax.broadcasted_iota(jnp.int32, (LANES, count), 0)
    stacked = jnp.where(
        line == 0,
        row_max,
        jnp.where(
            line == 1, 1.0 / total, jnp.where(line == 2, rest_max, top_sum / total / rest_sum)
        ),
    ).T
    tail = tail_ref[...]
    student = jnp.exp(logits_ref[...] - stacked[:, 0:1]) * stacked[:, 1:2]
    kept = enc_ref[...]
    chosen = kept >= 0.0
    spread = jnp.exp(jnp.where(chosen, -1e30, logits_ref[...]) - stacked[:, 2:3])
    grad = student * (1.0 - tail) + jnp.where(
        chosen, tail * student - kept, -(tail * stacked[:, 3:4]) * spread
    )
    grad_ref[...] = (LOSS_SCALE * grad).astype(BF16)
    for copy in copies:
        copy.wait_send()


def logit_gradient(nv, logits, enc, tail):
    count, width = logits.shape
    return pl.pallas_call(
        functools.partial(stats_kernel, nv),
        out_shape=jax.ShapeDtypeStruct((count, width), BF16),
        in_specs=[pl.BlockSpec(memory_space=VMEM)] * 3,
        out_specs=pl.BlockSpec(memory_space=VMEM),
        scratch_shapes=[
            VMEM((8, count), F32),
            VMEM((nv, 8, count), F32),
            DMA((nv,)), DMA((nv,)),
        ],
        compiler_params=params(1),
    )(logits, enc, tail)


def fold(nv, block, total, ybuf, zout, zbuf, ys, yr, zs, zr):
    z, y, along, partner = grid_peers(nv)
    nz = nv // 2
    order = list(range(1, nz)) + [0]
    copies = []
    for s in order:
        target = lax.rem(z + s, nz) * 2 + 1 - y
        copy = remote(block(target), ybuf.at[s], ys.at[s], yr.at[s], partner)
        copy.start()
        copies.append(copy)
    for s in order:
        remote(ybuf.at[s], ybuf.at[s], ys.at[s], yr.at[s], partner).wait_recv()
        own = block(lax.rem(z + s, nz) * 2 + y)[...]
        pair = own.astype(F32) + ybuf[s].astype(F32)
        if s == 0:
            total[...] = pair
        else:
            zout[s - 1] = pair.astype(BF16)
            copy = remote(
                zout.at[s - 1], zbuf.at[s - 1], zs.at[s - 1], zr.at[s - 1], along[s - 1]
            )
            copy.start()
            copies.append(copy)
    for s in range(1, nz):
        remote(
            zout.at[s - 1], zbuf.at[s - 1], zs.at[s - 1], zr.at[s - 1], along[s - 1]
        ).wait_recv()
        total[...] += zbuf[s - 1].astype(F32)
    for copy in copies:
        copy.wait_send()


def swap_pair(nd, nv):
    d = lax.axis_index("dp")
    v = lax.axis_index("vocab")
    c = nv // nd
    pair = {"dp": v // c, "vocab": d * c + lax.rem(v, c)}
    return pair, d != v // c


def swap(nd, nv, source, dest, send, recv):
    pair, other = swap_pair(nd, nv)

    @pl.when(other)
    def _():
        copy = remote(source, dest, send, recv, pair)
        copy.start()
        copy.wait()

    @pl.when(jnp.logical_not(other))
    def _():
        dest[...] = source[...]


def fold_scratch(nv, rows, width):
    nz = nv // 2
    return [
        VMEM((rows, width), F32),
        VMEM((rows, width), BF16),
        VMEM((nz, rows, width), BF16),
        VMEM((nz, rows, width), BF16),
        VMEM((nz, rows, width), BF16),
        DMA((nz,)), DMA((nz,)), DMA((nz,)), DMA((nz,)),
        DMA, DMA,
    ]


def head_kernel(
    nd, nv, part_ref, piece_ref, cols_ref,
    total, held, ybuf, zout, zbuf, ys, yr, zs, zr, ps, pr, gzs, gzr, gys, gyr,
):
    _, _, along, partner = grid_peers(nv)
    v = lax.axis_index("vocab")
    c = nv // nd
    rows, width = piece_ref.shape
    greet(along + [partner, swap_pair(nd, nv)[0]])

    def block(k):
        return part_ref.at[:, pl.ds(pl.multiple_of(k * width, width), width)]

    def slot(k):
        return cols_ref.at[
            pl.ds(pl.multiple_of((k // c) * rows, rows), rows),
            pl.ds(pl.multiple_of(lax.rem(k, c) * width, width), width),
        ]

    fold(nv, block, total, ybuf, zout, zbuf, ys, yr, zs, zr)
    held[...] = total[...].astype(BF16)
    swap(nd, nv, held, piece_ref, ps, pr)
    copies = spread_start(nv, piece_ref, slot, gzs, gzr, gys, gyr)
    slot(v)[...] = piece_ref[...]
    for s in range(1, nv // 2):
        copies.append(spread_forward(nv, s, slot, gzs, gzr, gys, gyr))
    spread_finish(nv, copies, slot, gys, gyr)


def head_exchange(nd, nv, part):
    rows, full = part.shape
    width = full // nv
    nz = nv // 2
    return pl.pallas_call(
        functools.partial(head_kernel, nd, nv),
        out_shape=(
            jax.ShapeDtypeStruct((rows, width), BF16),
            jax.ShapeDtypeStruct((rows * nd, full // nd), BF16),
        ),
        in_specs=[pl.BlockSpec(memory_space=VMEM)],
        out_specs=(pl.BlockSpec(memory_space=VMEM),) * 2,
        scratch_shapes=fold_scratch(nv, rows, width)
        + [DMA((nz,)), DMA((nz,)), DMA((nz,)), DMA((nz,))],
        compiler_params=params(2),
    )(part)


def last_kernel(
    nd, nv, part_ref, piece_ref, out_ref,
    total, held, ybuf, zout, zbuf, ys, yr, zs, zr, ps, pr,
):
    _, _, along, partner = grid_peers(nv)
    c = nv // nd
    rows, width = piece_ref.shape
    greet(along + [partner, swap_pair(nd, nv)[0]])

    def block(k):
        return part_ref.at[
            pl.ds(pl.multiple_of((k // c) * rows, rows), rows),
            pl.ds(pl.multiple_of(lax.rem(k, c) * width, width), width),
        ]

    fold(nv, block, total, ybuf, zout, zbuf, ys, yr, zs, zr)
    held[...] = (total[...] + piece_ref[...].astype(F32)).astype(BF16)
    swap(nd, nv, held, out_ref, ps, pr)


def last_exchange(nd, nv, part, piece):
    rows, width = piece.shape
    return pl.pallas_call(
        functools.partial(last_kernel, nd, nv),
        out_shape=jax.ShapeDtypeStruct((rows, width), BF16),
        in_specs=[pl.BlockSpec(memory_space=VMEM)] * 2,
        out_specs=pl.BlockSpec(memory_space=VMEM),
        scratch_shapes=fold_scratch(nv, rows, width),
        compiler_params=params(3),
    )(part, piece)


CHUNKS = 4


def pair_sum_kernel(nd, part_ref, out_ref, cbuf, xout, xbuf, cs, cr, xs, xr, os, orr):
    d = lax.axis_index("dp")
    nx = nd // 2
    x, core = d // 2, lax.rem(d, 2)
    mate = {"dp": x * 2 + 1 - core}
    far = [{"dp": lax.rem(x + s, nx) * 2 + core} for s in range(1, nx)]
    greet([mate] + far)
    rows = part_ref.shape[0]
    half = rows // 2
    step = half // CHUNKS

    def span(which, k):
        return pl.ds(pl.multiple_of(which * half + k * step, step), step)

    copies = []
    for k in range(CHUNKS):
        copy = remote(part_ref.at[span(1 - core, k)], cbuf.at[k], cs.at[k], cr.at[k], mate)
        copy.start()
        copies.append(copy)
    for k in range(CHUNKS):
        remote(cbuf.at[k], cbuf.at[k], cs.at[k], cr.at[k], mate).wait_recv()
        pair = part_ref[span(core, k), :].astype(F32) + cbuf[k].astype(F32)
        xout[k] = pair.astype(BF16)
        for s in range(1, nx):
            copy = remote(
                xout.at[k], xbuf.at[s - 1, k], xs.at[s - 1, k], xr.at[s - 1, k], far[s - 1]
            )
            copy.start()
            copies.append(copy)
    for k in range(CHUNKS):
        pair = xout[k].astype(F32)
        for s in range(1, nx):
            remote(
                xout.at[k], xbuf.at[s - 1, k], xs.at[s - 1, k], xr.at[s - 1, k], far[s - 1]
            ).wait_recv()
            pair = pair + xbuf[s - 1, k].astype(F32)
        out_ref[span(core, k), :] = pair.astype(BF16)
        place = out_ref.at[span(core, k)]
        copy = remote(place, place, os.at[k], orr.at[k], mate)
        copy.start()
        copies.append(copy)
    for k in range(CHUNKS):
        place = out_ref.at[span(1 - core, k)]
        remote(place, place, os.at[k], orr.at[k], mate).wait_recv()
    for copy in copies:
        copy.wait_send()


def pair_sum(nd, part):
    rows, width = part.shape
    nx = nd // 2
    step = rows // 2 // CHUNKS
    return pl.pallas_call(
        functools.partial(pair_sum_kernel, nd),
        out_shape=jax.ShapeDtypeStruct((rows, width), BF16),
        in_specs=[pl.BlockSpec(memory_space=VMEM)],
        out_specs=pl.BlockSpec(memory_space=VMEM),
        scratch_shapes=[
            VMEM((CHUNKS, step, width), BF16),
            VMEM((CHUNKS, step, width), BF16),
            VMEM((nx - 1, CHUNKS, step, width), BF16),
            DMA((CHUNKS,)), DMA((CHUNKS,)),
            DMA((nx - 1, CHUNKS)), DMA((nx - 1, CHUNKS)),
            DMA((CHUNKS,)), DMA((CHUNKS,)),
        ],
        compiler_params=params(4),
    )(part)


def swiglu_grads(gate_act, up_act, down_grad):
    sigma = jax.nn.sigmoid(gate_act)
    gate_grad = (down_grad * up_act * sigma * (1.0 + gate_act * (1.0 - sigma))).astype(BF16)
    up_grad = (down_grad * gate_act * sigma).astype(BF16)
    return (gate_grad, up_grad)


def body(
    nd, nv,
    head_input, body_input, head_weight, gate_weight, up_weight, down_weight,
    tile_ids, tile_probs, tile_slot,
):
    vocab_rows = head_weight.shape[0]
    count = tile_slot.shape[0]
    m = head_input.shape[0]
    head_rows, cols, enc, tail = intake(
        nd, nv, vocab_rows, head_input, body_input, tile_ids, tile_probs, tile_slot
    )
    every = lax.all_gather(cols, "vocab", axis=0)
    body_cols = every.transpose(1, 0, 2, 3).reshape(nd * nv * m, -1)
    gate_part = jnp.dot(body_cols, gate_weight, preferred_element_type=F32).astype(BF16)
    up_part = jnp.dot(body_cols, up_weight, preferred_element_type=F32).astype(BF16)
    gate_act = lax.psum(gate_part, "dp").astype(F32)
    up_act = lax.psum(up_part, "dp").astype(F32)

    head_rows = head_rows.reshape(count, -1)
    enc = enc.reshape(count, vocab_rows)
    logits = jnp.einsum("rd,vd->rv", head_rows, head_weight, preferred_element_type=F32)
    logit_grad = logit_gradient(nv, logits, enc, tail)
    partial = jnp.dot(logit_grad, head_weight, preferred_element_type=F32).astype(BF16)
    piece, grad_cols = head_exchange(nd, nv, partial)
    down_part = jnp.dot(grad_cols, down_weight, preferred_element_type=F32).astype(BF16)
    down_grad = pair_sum(nd, down_part).astype(F32)
    gate_grad, up_grad = swiglu_grads(gate_act, up_act, down_grad)
    slice_grad = jnp.einsum("rf,df->rd", gate_grad, gate_weight, preferred_element_type=F32)
    slice_grad = (
        slice_grad + jnp.einsum("rf,df->rd", up_grad, up_weight, preferred_element_type=F32)
    ).astype(BF16)
    return last_exchange(nd, nv, slice_grad, piece)


def solution(mesh):
    nd, nv = mesh.shape["dp"], mesh.shape["vocab"]
    return jax.shard_map(
        functools.partial(body, nd, nv),
        mesh=mesh,
        in_specs=(
            P(("dp", "vocab"), None),
            P(("dp", "vocab"), None),
            P("vocab", None),
            P("dp", "vocab"),
            P("dp", "vocab"),
            P("dp", "vocab"),
            P(("dp", "vocab"), None),
            P(("dp", "vocab"), None),
            P("dp"),
        ),
        out_specs=P("dp", "vocab"),
        check_vma=False,
    )
```

```python
import functools

import jax
import jax.numpy as jnp
from jax import lax
from jax.experimental import pallas as pl
from jax.experimental.pallas import tpu as pltpu
from jax.sharding import PartitionSpec as P

LOSS_SCALE = 1024
LANES = 128
TILE = 256
MESH = pl.DeviceIdType.MESH
VMEM = pltpu.VMEM
F32 = jnp.float32
BF16 = jnp.bfloat16
DMA = pltpu.SemaphoreType.DMA


def params(ident, mib=48):
    return pltpu.CompilerParams(
        collective_id=ident, has_side_effects=True, vmem_limit_bytes=mib * 1024 * 1024
    )


def remote(src, dst, send, recv, where):
    return pltpu.make_async_remote_copy(
        src_ref=src,
        dst_ref=dst,
        send_sem=send,
        recv_sem=recv,
        device_id=where,
        device_id_type=MESH,
    )


def greet(peers):
    barrier = pltpu.get_barrier_semaphore()
    for peer in peers:
        pl.semaphore_signal(barrier, inc=1, device_id=peer, device_id_type=MESH)
    pl.semaphore_wait(barrier, len(peers))


def grid_peers(nv):
    v = lax.axis_index("vocab")
    nz = nv // 2
    z, y = v // 2, lax.rem(v, 2)
    along = [{"vocab": lax.rem(z + s, nz) * 2 + y} for s in range(1, nz)]
    return z, y, along, {"vocab": z * 2 + 1 - y}


def spread_start(nv, source, slot, zs, zr, ys, yr):
    z, y, along, partner = grid_peers(nv)
    mine = z * 2 + y
    near = remote(source, slot(mine), ys.at[0], yr.at[0], partner)
    first = remote(source, slot(mine), zs.at[0], zr.at[0], along[0])
    first.start()
    near.start()
    return [first], [near]


def spread_forward(nv, s, source, slot, copies, zs, zr, ys, yr):
    z, y, along, partner = grid_peers(nv)
    nz = nv // 2
    mine = z * 2 + y
    rows, pairs = copies
    rows[-1].wait_send()
    if s + 1 < nz:
        copy = remote(source, slot(mine), zs.at[s], zr.at[s], along[s])
        copy.start()
        rows.append(copy)
    came = lax.rem(z - s + nz, nz) * 2 + y
    remote(slot(came), slot(came), zs.at[s - 1], zr.at[s - 1], along[s - 1]).wait_recv()
    copy = remote(slot(came), slot(came), ys.at[s], yr.at[s], partner)
    copy.start()
    pairs.append(copy)


def spread_finish(nv, copies, slot, ys, yr):
    z, y, _, partner = grid_peers(nv)
    nz = nv // 2
    for s in range(nz):
        theirs = lax.rem(z - s + nz, nz) * 2 + 1 - y
        remote(slot(theirs), slot(theirs), ys.at[s], yr.at[s], partner).wait_recv()
    for copy in copies[1]:
        copy.wait_send()


def cross_kernel(nd, body_ref, cols_ref, bs, br):
    d = lax.axis_index("dp")
    width = body_ref.shape[1] // nd
    others = [{"dp": lax.rem(d + s, nd)} for s in range(1, nd)]
    greet(others)
    copies = []
    for s in range(1, nd):
        to = lax.rem(d + s, nd)
        part = body_ref.at[:, pl.ds(pl.multiple_of(to * width, width), width)]
        copies.append(remote(part, cols_ref.at[d], bs.at[s - 1], br.at[s - 1], others[s - 1]))
    for copy in copies:
        copy.start()
    cols_ref[d] = body_ref[:, pl.ds(pl.multiple_of(d * width, width), width)]
    for s in range(1, nd):
        came = lax.rem(d - s + nd, nd)
        remote(
            cols_ref.at[came], cols_ref.at[came], bs.at[s - 1], br.at[s - 1], others[0]
        ).wait_recv()
    for copy in copies:
        copy.wait_send()


def cross(nd, body_input):
    m, width = body_input.shape
    return pl.pallas_call(
        functools.partial(cross_kernel, nd),
        out_shape=jax.ShapeDtypeStruct((nd, m, width // nd), BF16),
        in_specs=[pl.BlockSpec(memory_space=VMEM)],
        out_specs=pl.BlockSpec(memory_space=VMEM),
        scratch_shapes=[DMA((nd,)), DMA((nd,))],
        compiler_params=params(5),
    )(body_input)


def intake_kernel(
    nv, vocab_rows,
    head_ref, ids_ref, probs_ref, slot_ref,
    rows_ref, enc_ref, tail_ref,
    ids_all, probs_all, hi_s, lo_s, p_s,
    hzs, hzr, hys, hyr, ts, tr, us, ur,
):
    v = lax.axis_index("vocab")
    nz = nv // 2
    z, y, along, partner = grid_peers(nv)
    everyone = [{"vocab": lax.rem(v + s, nv)} for s in range(1, nv)]
    greet(everyone)
    small = []
    for s in range(1, nv):
        small.append(remote(ids_ref, ids_all.at[v], ts.at[s - 1], tr.at[s - 1], everyone[s - 1]))
        small.append(
            remote(probs_ref, probs_all.at[v], us.at[s - 1], ur.at[s - 1], everyone[s - 1])
        )
    for copy in small:
        copy.start()
    heads = spread_start(nv, head_ref, lambda k: rows_ref.at[k], hzs, hzr, hys, hyr)
    rows_ref[v] = head_ref[...]
    ids_all[v] = ids_ref[...]
    probs_all[v] = probs_ref[...]
    for s in range(1, nv):
        came = lax.rem(v - s + nv, nv)
        remote(ids_ref, ids_all.at[came], ts.at[s - 1], tr.at[s - 1], everyone[0]).wait_recv()
        remote(probs_ref, probs_all.at[came], us.at[s - 1], ur.at[s - 1], everyone[0]).wait_recv()

    count = slot_ref.shape[0]
    slots = ids_ref.shape[0]
    hi = jnp.zeros((count, LANES), F32)
    lo = jnp.zeros((count, LANES), F32)
    pr = jnp.zeros((count, LANES), F32)
    wanted = slot_ref[...]
    place = lax.broadcasted_iota(jnp.int32, (count, slots), 1)
    for k in range(nv):
        pick = jnp.where(place + k * slots == wanted, 1.0, 0.0).astype(BF16)
        ids = ids_all[k]
        top = lax.shift_right_logical(ids, 7).astype(F32).astype(BF16)
        low = lax.bitwise_and(ids, 127).astype(F32).astype(BF16)
        hi = hi + jnp.dot(pick, top, preferred_element_type=F32)
        lo = lo + jnp.dot(pick, low, preferred_element_type=F32)
        pr = pr + jnp.dot(pick, probs_all[k], preferred_element_type=F32)
    tail_ref[...] = 1.0 - jnp.sum(pr, axis=1, keepdims=True)
    nh = vocab_rows // LANES
    hi_s[...] = hi - (v * nh).astype(F32)
    lo_s[...] = lo
    p_s[...] = pr
    up_high = lax.broadcasted_iota(jnp.int32, (nh, LANES), 0).astype(F32)
    up_low = lax.broadcasted_iota(jnp.int32, (LANES, LANES), 0).astype(F32)

    def eight(step, carry):
        at = pl.multiple_of(step * 8, 8)
        hi8 = hi_s[pl.ds(at, 8), :]
        lo8 = lo_s[pl.ds(at, 8), :]
        p8 = p_s[pl.ds(at, 8), :]
        for j in range(8):
            hot = up_high == hi8[j : j + 1]
            low = jnp.where(up_low == lo8[j : j + 1], 1.0, 0.0).astype(BF16)
            both = jnp.concatenate(
                [jnp.where(hot, p8[j : j + 1], 0.0), jnp.where(hot, 1.0, 0.0)], axis=0
            ).astype(BF16)
            found = lax.dot_general(
                both, low, (((1,), (1,)), ((), ())), preferred_element_type=F32
            )
            enc_ref[at + j] = jnp.where(found[nh:] > 0.5, found[:nh], -1.0)
        return carry

    steps = count // 8
    bounds = [steps * s // nz for s in range(nz + 1)]
    for s in range(nz):
        lax.fori_loop(bounds[s], bounds[s + 1], eight, 0)
        if s + 1 < nz:
            spread_forward(
                nv, s + 1, head_ref, lambda k: rows_ref.at[k], heads, hzs, hzr, hys, hyr
            )
    spread_finish(nv, heads, lambda k: rows_ref.at[k], hys, hyr)
    for copy in small:
        copy.wait_send()


def intake(nv, vocab_rows, head_input, ids, probs, slot):
    m, width = head_input.shape
    slots, k = ids.shape
    count = slot.shape[0]
    nz = nv // 2
    return pl.pallas_call(
        functools.partial(intake_kernel, nv, vocab_rows),
        out_shape=(
            jax.ShapeDtypeStruct((nv, m, width), BF16),
            jax.ShapeDtypeStruct((count, vocab_rows // LANES, LANES), F32),
            jax.ShapeDtypeStruct((count, 1), F32),
        ),
        in_specs=[pl.BlockSpec(memory_space=VMEM)] * 4,
        out_specs=(pl.BlockSpec(memory_space=VMEM),) * 3,
        scratch_shapes=[
            VMEM((nv, slots, k), jnp.int32),
            VMEM((nv, slots, k), BF16),
            VMEM((count, k), F32),
            VMEM((count, k), F32),
            VMEM((count, k), F32),
            DMA((nz,)), DMA((nz,)), DMA((nz,)), DMA((nz,)),
            DMA((nv,)), DMA((nv,)), DMA((nv,)), DMA((nv,)),
        ],
        compiler_params=params(0),
    )(head_input, ids, probs, slot[:, None])


def stats_kernel(nv, logits_ref, enc_ref, tail_ref, grad_ref, mine, got, ss, sr):
    v = lax.axis_index("vocab")
    everyone = [{"vocab": lax.rem(v + s, nv)} for s in range(1, nv)]
    greet(everyone)
    count = logits_ref.shape[0]
    logits = logits_ref[...]
    picked = enc_ref[...] >= 0.0
    top_max = jnp.max(logits, axis=1, keepdims=True)
    rest = jnp.where(picked, -1e30, logits)
    low_max = jnp.max(rest, axis=1, keepdims=True)
    top = jnp.sum(jnp.where(picked, jnp.exp(logits - top_max), 0.0), axis=1, keepdims=True)
    low = jnp.sum(jnp.where(picked, 0.0, jnp.exp(rest - low_max)), axis=1, keepdims=True)
    lane = lax.broadcasted_iota(jnp.int32, (count, LANES), 1)
    packed = jnp.where(
        lane == 0, top_max, jnp.where(lane == 1, top, jnp.where(lane == 2, low_max, low))
    )
    mine[...] = packed.T[0:8]
    got[v] = mine[...]
    copies = [
        remote(mine, got.at[v], ss.at[s - 1], sr.at[s - 1], everyone[s - 1])
        for s in range(1, nv)
    ]
    for copy in copies:
        copy.start()
    for s in range(1, nv):
        came = lax.rem(v - s + nv, nv)
        remote(mine, got.at[came], ss.at[s - 1], sr.at[s - 1], everyone[0]).wait_recv()
    every = [got[k] for k in range(nv)]
    row_max = functools.reduce(jnp.maximum, [e[0:1] for e in every])
    rest_max = functools.reduce(jnp.maximum, [e[2:3] for e in every])
    top_sum = sum(e[1:2] * jnp.exp(e[0:1] - row_max) for e in every)
    rest_sum = sum(e[3:4] * jnp.exp(e[2:3] - rest_max) for e in every)
    total = top_sum + rest_sum * jnp.exp(rest_max - row_max)
    line = lax.broadcasted_iota(jnp.int32, (LANES, count), 0)
    stacked = jnp.where(
        line == 0,
        row_max,
        jnp.where(
            line == 1, 1.0 / total, jnp.where(line == 2, rest_max, top_sum / total / rest_sum)
        ),
    ).T
    tail = tail_ref[...]
    student = jnp.exp(logits_ref[...] - stacked[:, 0:1]) * stacked[:, 1:2]
    kept = enc_ref[...]
    chosen = kept >= 0.0
    spread = jnp.exp(jnp.where(chosen, -1e30, logits_ref[...]) - stacked[:, 2:3])
    grad = student * (1.0 - tail) + jnp.where(
        chosen, tail * student - kept, -(tail * stacked[:, 3:4]) * spread
    )
    grad_ref[...] = (LOSS_SCALE * grad).astype(BF16)
    for copy in copies:
        copy.wait_send()


def logit_gradient(nv, logits, enc, tail):
    count, width = logits.shape
    return pl.pallas_call(
        functools.partial(stats_kernel, nv),
        out_shape=jax.ShapeDtypeStruct((count, width), BF16),
        in_specs=[pl.BlockSpec(memory_space=VMEM)] * 3,
        out_specs=pl.BlockSpec(memory_space=VMEM),
        scratch_shapes=[
            VMEM((8, count), F32),
            VMEM((nv, 8, count), F32),
            DMA((nv,)), DMA((nv,)),
        ],
        compiler_params=params(1),
    )(logits, enc, tail)


def fold_order(nv):
    return list(range(1, nv // 2)) + [0]


def fold(nv, give, own, total, ybuf, zout, zbuf, ys, yr, zs, zr, make=lambda t: None):
    _, _, along, partner = grid_peers(nv)
    nz = nv // 2
    order = fold_order(nv)
    across = [remote(give(k), ybuf.at[k], ys.at[k], yr.at[k], partner) for k in range(nz)]
    copies = []
    make(0)
    across[0].start()
    for t in range(1, nz + 1):
        make(t)
    for k, s in enumerate(order):
        across[k].wait()
        if k + 1 < nz:
            across[k + 1].start()
        pair = own(k)[...].astype(F32) + ybuf[k].astype(F32)
        if s == 0:
            total[...] = pair
        else:
            zout[s - 1] = pair.astype(BF16)
            copy = remote(
                zout.at[s - 1], zbuf.at[s - 1], zs.at[s - 1], zr.at[s - 1], along[s - 1]
            )
            copy.start()
            copies.append(copy)
        if k + 1 < nz:
            make(nz + k + 1)
    for copy in copies:
        copy.wait()
    for s in range(1, nz):
        total[...] += zbuf[s - 1].astype(F32)


def swap_pair(nd, nv):
    d = lax.axis_index("dp")
    v = lax.axis_index("vocab")
    c = nv // nd
    pair = {"dp": v // c, "vocab": d * c + lax.rem(v, c)}
    return pair, d != v // c


def swap(nd, nv, source, dest, send, recv):
    pair, other = swap_pair(nd, nv)

    @pl.when(other)
    def _():
        copy = remote(source, dest, send, recv, pair)
        copy.start()
        copy.wait()

    @pl.when(jnp.logical_not(other))
    def _():
        dest[...] = source[...]


def fold_scratch(nv, rows, width):
    nz = nv // 2
    return [
        VMEM((rows, width), F32),
        VMEM((rows, width), BF16),
        VMEM((nz, rows, width), BF16),
        VMEM((nz, rows, width), BF16),
        VMEM((nz, rows, width), BF16),
        DMA((nz,)), DMA((nz,)), DMA((nz,)), DMA((nz,)),
        DMA, DMA,
    ]


def head_kernel(
    nd, nv, grad_ref, weight_ref, piece_ref, cols_ref,
    part, wbuf, ws,
    total, held, ybuf, zout, zbuf, ys, yr, zs, zr, ps, pr, gzs, gzr, gys, gyr,
):
    z, y, along, partner = grid_peers(nv)
    v = lax.axis_index("vocab")
    c = nv // nd
    nz = nv // 2
    rows, width = piece_ref.shape
    order = fold_order(nv)

    def fetch(t):
        side = 1 - y if t < nz else y
        target = lax.rem(z + order[t % nz], nz) * 2 + side
        return pltpu.make_async_copy(
            weight_ref.at[:, pl.ds(pl.multiple_of(target * width, width), width)],
            wbuf.at[t % 2],
            ws.at[t % 2],
        )

    def make(t):
        fetch(t).wait()
        if t + 1 < nv:
            fetch(t + 1).start()

        def tile(i, carry):
            at = pl.ds(pl.multiple_of(i * TILE, TILE), TILE)
            part[t, :, at] = jnp.dot(
                grad_ref[...], wbuf[t % 2, :, at], preferred_element_type=F32
            ).astype(BF16)
            return carry

        lax.fori_loop(0, width // TILE, tile, 0)

    def slot(k):
        return cols_ref.at[
            pl.ds(pl.multiple_of((k // c) * rows, rows), rows),
            pl.ds(pl.multiple_of(lax.rem(k, c) * width, width), width),
        ]

    fetch(0).start()
    greet(along + [partner, swap_pair(nd, nv)[0]])
    fold(
        nv, lambda k: part.at[k], lambda k: part.at[nz + k],
        total, ybuf, zout, zbuf, ys, yr, zs, zr, make,
    )
    held[...] = total[...].astype(BF16)
    swap(nd, nv, held, piece_ref, ps, pr)
    copies = spread_start(nv, piece_ref, slot, gzs, gzr, gys, gyr)
    slot(v)[...] = piece_ref[...]
    for s in range(1, nz):
        spread_forward(nv, s, piece_ref, slot, copies, gzs, gzr, gys, gyr)
    spread_finish(nv, copies, slot, gys, gyr)


def head_exchange(nd, nv, grad, weight):
    rows, depth = grad.shape
    full = weight.shape[1]
    width = full // nv
    nz = nv // 2
    return pl.pallas_call(
        functools.partial(head_kernel, nd, nv),
        out_shape=(
            jax.ShapeDtypeStruct((rows, width), BF16),
            jax.ShapeDtypeStruct((rows * nd, full // nd), BF16),
        ),
        in_specs=[pl.BlockSpec(memory_space=VMEM), pl.BlockSpec(memory_space=pl.ANY)],
        out_specs=(pl.BlockSpec(memory_space=VMEM),) * 2,
        scratch_shapes=[
            VMEM((nv, rows, width), BF16),
            VMEM((2, depth, width), BF16),
            DMA((2,)),
        ]
        + fold_scratch(nv, rows, width)
        + [DMA((nz,)), DMA((nz,)), DMA((nz,)), DMA((nz,))],
        compiler_params=params(2),
    )(grad, weight)


def last_kernel(
    nd, nv, part_ref, piece_ref, out_ref,
    total, held, ybuf, zout, zbuf, ys, yr, zs, zr, ps, pr,
):
    z, y, along, partner = grid_peers(nv)
    c = nv // nd
    nz = nv // 2
    order = fold_order(nv)
    rows, width = piece_ref.shape
    greet(along + [partner, swap_pair(nd, nv)[0]])

    def block(k):
        return part_ref.at[
            pl.ds(pl.multiple_of((k // c) * rows, rows), rows),
            pl.ds(pl.multiple_of(lax.rem(k, c) * width, width), width),
        ]

    fold(
        nv,
        lambda k: block(lax.rem(z + order[k], nz) * 2 + 1 - y),
        lambda k: block(lax.rem(z + order[k], nz) * 2 + y),
        total, ybuf, zout, zbuf, ys, yr, zs, zr,
    )
    held[...] = (total[...] + piece_ref[...].astype(F32)).astype(BF16)
    swap(nd, nv, held, out_ref, ps, pr)


def last_exchange(nd, nv, part, piece):
    rows, width = piece.shape
    return pl.pallas_call(
        functools.partial(last_kernel, nd, nv),
        out_shape=jax.ShapeDtypeStruct((rows, width), BF16),
        in_specs=[pl.BlockSpec(memory_space=VMEM)] * 2,
        out_specs=pl.BlockSpec(memory_space=VMEM),
        scratch_shapes=fold_scratch(nv, rows, width),
        compiler_params=params(3),
    )(part, piece)


CHUNKS = 4


def pair_sum_kernel(nd, part_ref, out_ref, cbuf, xout, xbuf, cs, cr, xs, xr, os, orr):
    d = lax.axis_index("dp")
    nx = nd // 2
    x, core = d // 2, lax.rem(d, 2)
    mate = {"dp": x * 2 + 1 - core}
    far = [{"dp": lax.rem(x + s, nx) * 2 + core} for s in range(1, nx)]
    greet([mate] + far)
    rows = part_ref.shape[0]
    half = rows // 2
    step = half // CHUNKS

    def span(which, k):
        return pl.ds(pl.multiple_of(which * half + k * step, step), step)

    copies = []
    for k in range(CHUNKS):
        copy = remote(part_ref.at[span(1 - core, k)], cbuf.at[k], cs.at[k], cr.at[k], mate)
        copy.start()
        copies.append(copy)
    for k in range(CHUNKS):
        remote(cbuf.at[k], cbuf.at[k], cs.at[k], cr.at[k], mate).wait_recv()
        pair = part_ref[span(core, k), :].astype(F32) + cbuf[k].astype(F32)
        xout[k] = pair.astype(BF16)
        for s in range(1, nx):
            copy = remote(
                xout.at[k], xbuf.at[s - 1, k], xs.at[s - 1, k], xr.at[s - 1, k], far[s - 1]
            )
            copy.start()
            copies.append(copy)
    for k in range(CHUNKS):
        pair = xout[k].astype(F32)
        for s in range(1, nx):
            remote(
                xout.at[k], xbuf.at[s - 1, k], xs.at[s - 1, k], xr.at[s - 1, k], far[s - 1]
            ).wait_recv()
            pair = pair + xbuf[s - 1, k].astype(F32)
        out_ref[span(core, k), :] = pair.astype(BF16)
        place = out_ref.at[span(core, k)]
        copy = remote(place, place, os.at[k], orr.at[k], mate)
        copy.start()
        copies.append(copy)
    for k in range(CHUNKS):
        place = out_ref.at[span(1 - core, k)]
        remote(place, place, os.at[k], orr.at[k], mate).wait_recv()
    for copy in copies:
        copy.wait_send()


def pair_sum(nd, part):
    rows, width = part.shape
    nx = nd // 2
    step = rows // 2 // CHUNKS
    return pl.pallas_call(
        functools.partial(pair_sum_kernel, nd),
        out_shape=jax.ShapeDtypeStruct((rows, width), BF16),
        in_specs=[pl.BlockSpec(memory_space=VMEM)],
        out_specs=pl.BlockSpec(memory_space=VMEM),
        scratch_shapes=[
            VMEM((CHUNKS, step, width), BF16),
            VMEM((CHUNKS, step, width), BF16),
            VMEM((nx - 1, CHUNKS, step, width), BF16),
            DMA((CHUNKS,)), DMA((CHUNKS,)),
            DMA((nx - 1, CHUNKS)), DMA((nx - 1, CHUNKS)),
            DMA((CHUNKS,)), DMA((CHUNKS,)),
        ],
        compiler_params=params(4),
    )(part)


def swiglu_grads(gate_act, up_act, down_grad):
    sigma = jax.nn.sigmoid(gate_act)
    gate_grad = (down_grad * up_act * sigma * (1.0 + gate_act * (1.0 - sigma))).astype(BF16)
    up_grad = (down_grad * gate_act * sigma).astype(BF16)
    return (gate_grad, up_grad)


def body(
    nd, nv,
    head_input, body_input, head_weight, gate_weight, up_weight, down_weight,
    tile_ids, tile_probs, tile_slot,
):
    vocab_rows = head_weight.shape[0]
    count = tile_slot.shape[0]
    m = head_input.shape[0]
    cols = cross(nd, body_input)
    cols, head_input = lax.optimization_barrier((cols, head_input))
    every = lax.all_gather(cols, "vocab", axis=0)
    head_rows, enc, tail = intake(nv, vocab_rows, head_input, tile_ids, tile_probs, tile_slot)
    head_rows = head_rows.reshape(count, -1)
    enc = enc.reshape(count, vocab_rows)
    logits = jnp.einsum("rd,vd->rv", head_rows, head_weight, preferred_element_type=F32)
    logit_grad = logit_gradient(nv, logits, enc, tail)
    every, logit_grad = lax.optimization_barrier((every, logit_grad))
    body_cols = every.transpose(1, 0, 2, 3).reshape(nd * nv * m, -1)
    gate_part = jnp.dot(body_cols, gate_weight, preferred_element_type=F32).astype(BF16)
    up_part = jnp.dot(body_cols, up_weight, preferred_element_type=F32).astype(BF16)
    gate_act = lax.psum(gate_part, "dp").astype(F32)
    up_act = lax.psum(up_part, "dp").astype(F32)
    piece, grad_cols = head_exchange(nd, nv, logit_grad, head_weight)
    down_part = jnp.dot(grad_cols, down_weight, preferred_element_type=F32).astype(BF16)
    down_grad = pair_sum(nd, down_part).astype(F32)
    gate_grad, up_grad = swiglu_grads(gate_act, up_act, down_grad)
    slice_grad = jnp.einsum("rf,df->rd", gate_grad, gate_weight, preferred_element_type=F32)
    slice_grad = (
        slice_grad + jnp.einsum("rf,df->rd", up_grad, up_weight, preferred_element_type=F32)
    ).astype(BF16)
    return last_exchange(nd, nv, slice_grad, piece)


def solution(mesh):
    nd, nv = mesh.shape["dp"], mesh.shape["vocab"]
    return jax.shard_map(
        functools.partial(body, nd, nv),
        mesh=mesh,
        in_specs=(
            P(("dp", "vocab"), None),
            P(("dp", "vocab"), None),
            P("vocab", None),
            P("dp", "vocab"),
            P("dp", "vocab"),
            P("dp", "vocab"),
            P(("dp", "vocab"), None),
            P(("dp", "vocab"), None),
            P("dp"),
        ),
        out_specs=P("dp", "vocab"),
        check_vma=False,
    )
```
